32 devices in a mesh: gx: 4 (over y, x), gy: 8 (over z, core).
Axes of the slice: x: 2, y: 2, z: 4, core: 2. Of those that a mesh axis runs over, the one named last changes fastest.
Arguments:
- prior_acoustic_field: bfloat16 [96, 49152], P('gx', 'gy'), may hold values from -6 to 6
- opening_acoustic_field: bfloat16 [96, 49152], P('gx', 'gy'), may hold values from -6 to 6
- courant_coefficient: bfloat16 [96, 49152], P('gx', 'gy'), may hold values from 0.019897461 to 0.119628906
- pulse_shape: float32 [2], replicated, may hold values from -8 to 8
- emitter_coordinates: int32 [128, 2], P(('gx', 'gy')), may hold values from 0 to 191, as said below
- emission_instant: int32 [128], P(('gx', 'gy')), may hold values from 0 to 1
- captured_waveforms: float32 [2, 128], P(None, ('gx', 'gy')), may hold values from -6 to 6
Outputs:
- gradient: float32 [96, 49152], P('gx', 'gy')
- residual_traces: float32 [2, 128], P(None, ('gx', 'gy'))
The draws below stay inside these ranges and needn't reach their ends.
Inputs may be any that keep to these rules, and one draw needn't show every extreme that they name: `emitter_coordinates`: first column below 96, second below 192; several elements may share a cell.
All inputs are finite; a program needn't handle non-finite values.
Results may differ from the reference program's by a relative error of at most 0.0003.
Values sent between devices are 32-bit elements; how exact they have to be, the bound alone decides.
A program may use at most 128 MiB of HBM per device.

```python
import math
import jax
import jax.numpy as jnp
from jax import lax

CX = 24
CY = 24
HALO = 8
SPAN = 40
DEPTH = 256
MARCH_COUNT = 2
TRANSDUCER_COUNT = 128
NX = 96
NY = 192


def draw_emitter_coordinates(key, part):
    key = jax.random.fold_in(key, 7)
    row_key, column_key = jax.random.split(key)
    across = jax.random.randint(row_key, (TRANSDUCER_COUNT,), 0, NX, dtype=jnp.int32)
    along = jax.random.randint(column_key, (TRANSDUCER_COUNT,), 0, NY, dtype=jnp.int32)
    across = across.at[0].set(NX - 1).at[1].set(0)
    along = along.at[0].set(NY - 1).at[1].set(0)
    return jnp.stack([across, along], axis=1)


def with_ends(drawn, key, least, largest):
    index_at = [jax.random.randint(jax.random.fold_in(key, axis), (), 0, length) for axis, length in enumerate(drawn.shape)]
    main_axis = drawn.shape.index(max(drawn.shape))
    beside = index_at[:main_axis] + [(index_at[main_axis] + 1) % drawn.shape[main_axis]] + index_at[main_axis + 1:]
    return drawn.at[tuple(index_at)].set(least).at[tuple(beside)].set(largest)


def level_of(rng, extent, cuts, smallest, top_value):
    def one(dim, parts):
        heights = jax.random.uniform(jax.random.fold_in(jax.random.fold_in(rng, 6), dim), (parts,), jnp.float32, smallest / len(cuts), top_value / len(cuts))
        return jnp.repeat(jnp.exp(heights), extent[dim] // parts).reshape((-1,) + (1,) * (len(extent) - dim - 1))

    level = one(*cuts[0])
    for cut in cuts[1:]:
        level = level * one(*cut)
    return level


def normal_values(own_key, dims, deviation, reach, shards=(), kind=jnp.bfloat16):
    drawn = deviation * jax.random.normal(own_key, dims, jnp.float32)
    if shards:
        drawn = drawn * level_of(own_key, dims, shards, -0.22, 0.18)
    return jnp.clip(drawn, -reach, reach).astype(kind)


def setup_inputs(seed: int = 0) -> dict:
    seeds = jax.random.split(jax.random.key(seed), 8)
    prior_acoustic_field = normal_values(seeds[0], (NX, NY * DEPTH), 1.0, 6.0, ((0, 4), (1, 8)))
    opening_acoustic_field = normal_values(seeds[1], (NX, NY * DEPTH), 1.0, 6.0, ((0, 4), (1, 8)))
    courant_coefficient = jnp.clip(jnp.exp(math.log(0.119628906) - 1.7938024 * jax.random.uniform(seeds[2], (NX, NY * DEPTH), jnp.float32) ** level_of(seeds[2], (NX, NY * DEPTH), ((0, 4), (1, 8)), -0.2, 0.2)), 0.019897461, 0.119628906).astype(jnp.bfloat16)
    pulse_shape = normal_values(seeds[3], (MARCH_COUNT,), 2.0, 8.0, (), jnp.float32)
    emitter_coordinates = draw_emitter_coordinates(jax.random.fold_in(seeds[7], 71), 0)
    emission_instant = with_ends(jax.random.randint(seeds[5], (TRANSDUCER_COUNT,), 0, MARCH_COUNT), jax.random.fold_in(seeds[5], 1), 0, MARCH_COUNT - 1).astype(jnp.int32)
    captured_waveforms = normal_values(seeds[6], (MARCH_COUNT, TRANSDUCER_COUNT), 1.0, 6.0, ((1, 32),), jnp.float32)
    return {"prior_acoustic_field": prior_acoustic_field, "opening_acoustic_field": opening_acoustic_field, "courant_coefficient": courant_coefficient, "pulse_shape": pulse_shape, "emitter_coordinates": emitter_coordinates, "emission_instant": emission_instant, "captured_waveforms": captured_waveforms}


def lateral_kernel(span_cells, row_count, rim_width):
    counter = jnp.arange(span_cells, dtype=jnp.int32)
    product = counter[:, None] * counter[None, :] % span_cells
    angles = 2.0 * math.pi / span_cells * product.astype(jnp.float32)
    cosine = jnp.cos(angles)
    sines = jnp.sin(angles)
    wavenums = jnp.where(counter <= span_cells // 2, counter, counter - span_cells).astype(jnp.float32)
    weight = -(2.0 * math.pi / span_cells * wavenums) ** 2 / span_cells
    full = jnp.dot(cosine * weight[None, :], cosine.T, precision=lax.Precision.HIGHEST)
    full = full + jnp.dot(sines * weight[None, :], sines.T, precision=lax.Precision.HIGHEST)
    return full[rim_width:rim_width + row_count]

def depth_kernel(depth_cells):
    counter = jnp.arange(depth_cells, dtype=jnp.int32) + 1
    product = counter[:, None] * counter[None, :] % (2 * (depth_cells + 1))
    sines = math.sqrt(2.0 / (depth_cells + 1)) * jnp.sin(math.pi / (depth_cells + 1) * product.astype(jnp.float32))
    weight = -(math.pi / (depth_cells + 1) * counter.astype(jnp.float32)) ** 2
    return jnp.dot(sines * weight[None, :], sines.T, precision=lax.Precision.HIGHEST)

def laplacian(wavefield, kernel_lateral, kernel_depth):
    padded = jnp.pad(wavefield, ((HALO, HALO), (HALO, HALO), (0, 0)))
    zero_index = jnp.zeros((), jnp.int32)
    rim_index = zero_index + HALO

    def first_block(block_index):
        window = lax.dynamic_slice(padded, (block_index * CX, rim_index, zero_index), (SPAN, NY, DEPTH))
        return jnp.einsum('ab,bcz->acz', kernel_lateral, window, precision=lax.Precision.HIGHEST)

    def second_block(block_index):
        window = lax.dynamic_slice(padded, (rim_index, block_index * CY, zero_index), (NX, SPAN, DEPTH))
        return jnp.einsum('cd,adz->acz', kernel_lateral, window, precision=lax.Precision.HIGHEST)
    first_part = lax.map(first_block, jnp.arange(NX // CX, dtype=jnp.int32)).reshape(NX, NY, DEPTH)
    second_part = lax.map(second_block, jnp.arange(NY // CY, dtype=jnp.int32))
    second_part = jnp.transpose(second_part, (1, 0, 2, 3)).reshape(NX, NY, DEPTH)
    depth_part = jnp.einsum('acz,zw->acw', wavefield, kernel_depth, precision=lax.Precision.HIGHEST)
    return first_part + second_part + depth_part

def reference(prior_acoustic_field, opening_acoustic_field, courant_coefficient, pulse_shape, emitter_coordinates, emission_instant, captured_waveforms):
    kernel_lateral = lateral_kernel(SPAN, CX, HALO)
    kernel_depth = depth_kernel(DEPTH)
    across = emitter_coordinates[:, 0]
    along = emitter_coordinates[:, 1]
    previous = prior_acoustic_field.astype(jnp.float32).reshape(NX, NY, DEPTH)
    current = opening_acoustic_field.astype(jnp.float32).reshape(NX, NY, DEPTH)
    stiff_values = courant_coefficient.astype(jnp.float32).reshape(NX, NY, DEPTH)
    images = []
    records = []
    for instant_amount in range(MARCH_COUNT):
        laplace_out = laplacian(current, kernel_lateral, kernel_depth)
        images.append(laplace_out)
        emitter_excitation = pulse_shape[instant_amount] * (emission_instant == instant_amount).astype(jnp.float32)
        planes = jnp.zeros((NX, NY), jnp.float32).at[across, along].add(emitter_excitation)
        newest = 2.0 * current - previous + stiff_values * laplace_out
        newest = newest.at[:, :, 0].add(planes)
        records.append(newest[across, along, 0])
        previous, current = (current, newest)
    residual_traces = jnp.stack(records) - captured_waveforms
    later_field = jnp.zeros((NX, NY, DEPTH), jnp.float32)
    adjoint = jnp.zeros((NX, NY, DEPTH), jnp.float32)
    gradient = jnp.zeros((NX, NY, DEPTH), jnp.float32)
    for instant_amount in reversed(range(MARCH_COUNT)):
        planes = jnp.zeros((NX, NY), jnp.float32).at[across, along].add(residual_traces[instant_amount])
        newest = 2.0 * adjoint - later_field
        if instant_amount < MARCH_COUNT - 1:
            newest = newest + stiff_values * laplacian(adjoint, kernel_lateral, kernel_depth)
        newest = newest.at[:, :, 0].add(planes)
        gradient = gradient + newest * images[instant_amount]
        later_field, adjoint = (adjoint, newest)
    return (gradient.reshape(NX, NY * DEPTH), residual_traces)
```

```python
import functools

import jax
import jax.numpy as jnp
import ml_dtypes
import numpy as np
from jax import lax
from jax.experimental import pallas as pl
from jax.experimental.pallas import tpu as pltpu
from jax.sharding import PartitionSpec as P

CX = 24
CY = 24
HALO = 8
SPAN = 40
DEPTH = 256
LANES = 128
MESH = pl.DeviceIdType.MESH
HIGH = lax.Precision.HIGHEST
F32 = jnp.float32
BF16 = jnp.bfloat16


def constants():
    k = np.arange(SPAN)
    w = np.where(k <= SPAN // 2, k, k - SPAN)
    diff = k[:, None] - k[None, :]
    kx = np.einsum(
        "k,abk->ab",
        -((2 * np.pi * w / SPAN) ** 2) / SPAN,
        np.cos(2 * np.pi * diff[:, :, None] * k / SPAN),
    )
    kc = kx[HALO : HALO + CX]
    n = np.arange(DEPTH) + 1
    s = np.sqrt(2 / (DEPTH + 1)) * np.sin(np.pi / (DEPTH + 1) * (n[:, None] * n[None, :]))
    kz = (s * -((np.pi * n / (DEPTH + 1)) ** 2)) @ s.T

    def halves(a):
        hi = a.astype(ml_dtypes.bfloat16)
        return hi, (a - hi.astype(np.float64)).astype(ml_dtypes.bfloat16)

    kz2 = np.concatenate(halves(kz), axis=0)
    kc2 = np.concatenate(halves(kc), axis=0)
    small = np.zeros((24 + 3 * LANES + 8, DEPTH), np.float32)
    small[:CX, :SPAN] = kc
    taps = small[24 : 24 + 3 * LANES]
    taps[0:CX, :CX] = kc[:, HALO : HALO + CX].T
    taps[LANES + CX - HALO : LANES + CX, :CX] = kc[:, :HALO].T
    taps[2 * LANES : 2 * LANES + HALO, :CX] = kc[:, HALO + CX :].T
    small[24 + 3 * LANES :] = kz[0]
    return kz2, kc2, small, float(kz[0, 0])


def kernel(
    nx, ny, kz00,
    prior_hbm, opening_hbm, courant_hbm, kz_hbm, kc_hbm, small_hbm,
    pulse, coords, instants, captured,
    grad_ref, resid_ref,
    prior, opening, courant, kz2, kc2, small,
    field, low_x, high_x, image,
    tiles_y, table, plane_ext, plane_low, plane_high, parts_x, parts_y, rec_out,
    load_sem, halo_send, halo_recv, ty_send, ty_recv, tx_send, tx_recv,
    rx_send, rx_recv, ry_send, ry_recv,
):
    gx, gy = lax.axis_index("gx"), lax.axis_index("gy")
    slots = instants.shape[0]

    loads = [
        pltpu.make_async_copy(src, dst, load_sem.at[i])
        for i, (src, dst) in enumerate(
            [
                (opening_hbm, opening), (kz_hbm, kz2), (kc_hbm, kc2),
                (prior_hbm, prior), (courant_hbm, courant), (small_hbm, small),
            ]
        )
    ]
    for load in loads:
        load.start()

    peers_y = [(gx, lax.rem(gy + k, ny)) for k in range(1, ny)]
    peers_x = [(lax.rem(gx + k, nx), gy) for k in range(1, nx)]
    barrier = pltpu.get_barrier_semaphore()
    for peer in peers_y + peers_x:
        pl.semaphore_signal(barrier, inc=1, device_id=peer, device_id_type=MESH)

    lane_row = lax.broadcasted_iota(jnp.int32, (ny, LANES), 1)
    sub_row = lax.broadcasted_iota(jnp.int32, (ny, LANES), 0)
    mine = jnp.zeros((ny, LANES), F32)
    for j in range(slots):
        values = [
            captured[0, j], captured[1, j], coords[j, 0].astype(F32), coords[j, 1].astype(F32),
            instants[j].astype(F32),
        ]
        for f, value in enumerate(values):
            mine = jnp.where(lane_row == f * slots + j, value, mine)
    tiles_y[gy] = jnp.where(sub_row == gy, mine, 0.0)

    loads[0].wait()
    for y in range(CY):
        for h in range(2):
            c0 = y * DEPTH + h * LANES
            field[h, HALO + y] = opening[:, c0 : c0 + LANES].astype(F32)

    pl.semaphore_wait(barrier, nx + ny - 2)

    def remote(src, dst, send, recv, peer):
        return pltpu.make_async_remote_copy(
            src_ref=src, dst_ref=dst, send_sem=send, recv_sem=recv,
            device_id=peer, device_id_type=MESH,
        )

    for _, py in peers_y:
        remote(tiles_y.at[gy], tiles_y.at[gy], ty_send.at[py], ty_recv.at[gy], (gx, py)).start()

    ends = [
        (gy > 0, (gx, lax.max(gy - 1, 0))),
        (gy < ny - 1, (gx, lax.min(gy + 1, ny - 1))),
        (gx > 0, (lax.max(gx - 1, 0), gy)),
        (gx < nx - 1, (lax.min(gx + 1, nx - 1), gy)),
    ]

    def swap(stage, sources, targets):
        for i in (2, 3, 0, 1):
            there, peer = ends[i]

            @pl.when(there)
            def _():
                remote(
                    sources[i], targets[i ^ 1], halo_send.at[stage, i],
                    halo_recv.at[stage, i ^ 1], peer,
                ).start()

            @pl.when(jnp.logical_not(there))
            def _():
                targets[i][...] = jnp.zeros(targets[i].shape, F32)

        def finish():
            for i in range(4):
                there, peer = ends[i]

                @pl.when(there)
                def _():
                    copy = remote(
                        sources[i], targets[i], halo_send.at[stage, i],
                        halo_recv.at[stage, i], peer,
                    )
                    copy.wait_recv()
                    copy.wait_send()

        return finish

    finish_halo = swap(
        0,
        [
            field.at[:, HALO : 2 * HALO], field.at[:, CY : CY + HALO],
            field.at[:, HALO : HALO + CY, 0:HALO], field.at[:, HALO : HALO + CY, CX - HALO : CX],
        ],
        [field.at[:, 0:HALO], field.at[:, HALO + CY :], low_x, high_x],
    )

    loads[1].wait()
    for b in range(3):
        rows = [field[h, HALO + 8 * b : 16 + 8 * b].reshape(8 * CX, LANES) for h in range(2)]
        lhs = jnp.concatenate(rows, axis=1).astype(BF16)
        out = jnp.dot(lhs, kz2[:DEPTH], preferred_element_type=F32)
        out = out + jnp.dot(lhs, kz2[DEPTH:], preferred_element_type=F32)
        for h in range(2):
            image[h, 8 * b * CX : 8 * (b + 1) * CX] = out[:, h * LANES : (h + 1) * LANES]

    for _, py in peers_y:
        copy = remote(tiles_y.at[gy], tiles_y.at[py], ty_send.at[py], ty_recv.at[py], (gx, py))
        copy.wait_recv()
        copy.wait_send()
    table[gx] = jnp.sum(tiles_y[...], axis=0)
    for px, _ in peers_x:
        remote(table.at[gx], table.at[gx], tx_send.at[px], tx_recv.at[gx], (px, gy)).start()
    for px, _ in peers_x:
        copy = remote(table.at[gx], table.at[px], tx_send.at[px], tx_recv.at[px], (px, gy))
        copy.wait_recv()
        copy.wait_send()

    devices = nx * ny
    elements = table[...].reshape(devices, LANES)
    lane = lax.broadcasted_iota(jnp.int32, (devices, LANES), 1)
    first_hits, second_hits, spread = [], [], []
    group = lane // CY
    for j in range(slots):
        def column(f):
            return elements[:, f * slots + j : f * slots + j + 1]

        x = column(2).astype(jnp.int32) - gx * CX
        y = column(3).astype(jnp.int32) - gy * CY
        fires = column(4)
        first_hits.append(jnp.where((lane == x) & (lane < CX), 1.0, 0.0))
        second_hits.append(jnp.where((lane == y) & (lane < CY), 1.0, 0.0))
        weight = jnp.where(group == 0, jnp.where(fires == 0.0, pulse[0], 0.0), 0.0)
        weight = jnp.where(group == 1, jnp.where(fires == 1.0, pulse[1], 0.0), weight)
        weight = jnp.where(group == 2, 1.0, weight)
        weight = jnp.where(group == 3, column(0), weight)
        weight = jnp.where(group == 4, column(1), weight)
        inside = (lane - group * CY == y)
        spread.append(jnp.where(inside, weight, 0.0))
    first_hits = jnp.concatenate(first_hits, axis=0)
    second_hits = jnp.concatenate(second_hits, axis=0)
    planes = lax.dot_general(
        jnp.concatenate(spread, axis=0), first_hits, (((0,), (0,)), ((), ())),
        precision=HIGH, preferred_element_type=F32,
    )
    source_0, source_1, hits, seen_0, seen_1 = [planes[CY * i : CY * (i + 1)] for i in range(5)]

    loads[2].wait()
    loads[3].wait()
    loads[4].wait()
    loads[5].wait()
    finish_halo()

    flat = field.reshape(2, SPAN * CX, LANES)
    kc = kc2[...]

    def lateral(window):
        out = jnp.dot(kc, window.astype(BF16), preferred_element_type=F32)
        return out[:CX] + out[CX:]

    def both(x):
        window = jnp.concatenate(
            [flat[h, pl.ds(x, SPAN, stride=CX), :] for h in range(2)], axis=1
        )
        out = lateral(window)
        for h in range(2):
            at = (h, pl.ds(x, CY, stride=CX), slice(None))
            image[at] = image[at] + out[:, h * LANES : (h + 1) * LANES]

    def first(y):
        window = jnp.concatenate(
            [
                jnp.concatenate([low_x[h, y], field[h, HALO + y], high_x[h, y]], axis=0)
                for h in range(2)
            ],
            axis=1,
        )
        out = lateral(window)
        for h in range(2):
            image[h, CX * y : CX * (y + 1)] += out[:, h * LANES : (h + 1) * LANES]

    for i in range(CX):
        both(i)
    for i in range(CY):
        first(i)

    diag = (
        lax.broadcasted_iota(jnp.int32, (8, CX, LANES), 1)
        == lax.broadcasted_iota(jnp.int32, (8, CX, LANES), 2)
    )

    def to_plane(columns):
        return jnp.sum(jnp.where(diag, columns, 0.0), axis=1)

    kz_row = [small[24 + 3 * LANES : 25 + 3 * LANES, h * LANES : (h + 1) * LANES] for h in range(2)]
    gathered = []
    for b in range(3):
        total = jnp.zeros((8, CX, LANES), F32)
        for h in range(2):
            def block(ref):
                return jnp.stack(
                    [
                        ref[:, y * DEPTH + h * LANES : y * DEPTH + (h + 1) * LANES].astype(F32)
                        for y in range(8 * b, 8 * b + 8)
                    ]
                )

            now = field[h, HALO + 8 * b : 16 + 8 * b]
            im = image[h, 8 * b * CX : 8 * (b + 1) * CX].reshape(8, CX, LANES)
            c = block(courant)
            newest = 2.0 * now - block(prior) + c * im
            total = total + newest * kz_row[h]
            if h == 0:
                tops = [newest[:, :, 0:1], now[:, :, 0:1], c[:, :, 0:1], im[:, :, 0:1]]
        tops.append(jnp.sum(total, axis=2, keepdims=True))
        gathered.append([to_plane(top) for top in tops])
    p1, p0, c0, im0, depth1 = [jnp.concatenate(rows, axis=0) for rows in zip(*gathered)]
    p1 = p1 + source_0
    depth1 = depth1 + kz00 * source_0

    def lateral_plane(stage, plane):
        ext, low, high = plane_ext.at[stage], plane_low.at[stage], plane_high.at[stage]
        ext[HALO : HALO + CY] = plane
        finish = swap(
            stage + 1,
            [
                ext.at[HALO : 2 * HALO], ext.at[CY : CY + HALO],
                ext.at[HALO : HALO + CY], ext.at[HALO : HALO + CY],
            ],
            [ext.at[0:HALO], ext.at[HALO + CY :], low, high],
        )

        def rest():
            finish()
            out = jnp.dot(small[:CX, :SPAN], ext[...], precision=HIGH, preferred_element_type=F32)
            wide = jnp.concatenate([plane, low[...], high[...]], axis=1)
            taps = small[24 : 24 + 3 * LANES, :LANES]
            return out + jnp.dot(wide, taps, precision=HIGH, preferred_element_type=F32)

        return rest

    im1 = lateral_plane(0, p1)() + depth1
    p2 = 2.0 * p1 - p0 + c0 * im1 + source_1
    a1 = hits * p2 - seen_1
    inject_0 = hits * p1 - seen_0
    finish_a1 = lateral_plane(1, a1)

    records = jnp.zeros((devices, LANES), F32)
    for t, plane in enumerate((p1, p2)):
        picked = jnp.dot(second_hits[:, :CY], plane, precision=HIGH, preferred_element_type=F32)
        picked = jnp.sum(picked * first_hits, axis=1, keepdims=True)
        for j in range(slots):
            records = jnp.where(
                lane == t * slots + j, picked[j * devices : (j + 1) * devices], records
            )
    rec_out[...] = records.reshape(nx, ny, LANES)
    parts_x[gx] = rec_out[gx]
    for px, _ in peers_x:
        remote(rec_out.at[px], parts_x.at[gx], rx_send.at[px], rx_recv.at[gx], (px, gy)).start()

    for b in range(3):
        columns = jnp.sum(
            jnp.where(diag, a1[8 * b : 8 * b + 8].reshape(8, 1, LANES), 0.0), axis=2, keepdims=True
        )
        for i in range(8):
            y = 8 * b + i
            for h in range(2):
                at = (slice(None), slice(y * DEPTH + h * LANES, y * DEPTH + (h + 1) * LANES))
                grad_ref[at] = (
                    courant[at].astype(F32) * (columns[i] * kz_row[h])
                    * image[h, y * CX : (y + 1) * CX]
                )

    for px, _ in peers_x:
        copy = remote(rec_out.at[px], parts_x.at[px], rx_send.at[px], rx_recv.at[px], (px, gy))
        copy.wait_recv()
        copy.wait_send()
    parts_y[gy] = jnp.sum(parts_x[...], axis=0)
    for _, py in peers_y:
        remote(parts_y.at[gy], parts_y.at[gy], ry_send.at[py], ry_recv.at[gy], (gx, py)).start()

    more = (2.0 * a1 + c0 * finish_a1() + inject_0) * im0 + a1 * im1
    top = lax.broadcasted_iota(jnp.int32, (CX, LANES), 1) == 0
    for b in range(3):
        columns = jnp.sum(
            jnp.where(diag, more[8 * b : 8 * b + 8].reshape(8, 1, LANES), 0.0),
            axis=2, keepdims=True,
        )
        for i in range(8):
            at = (slice(None), slice((8 * b + i) * DEPTH, (8 * b + i) * DEPTH + LANES))
            grad_ref[at] = grad_ref[at] + jnp.where(top, columns[i], 0.0)

    for _, py in peers_y:
        copy = remote(parts_y.at[gy], parts_y.at[py], ry_send.at[py], ry_recv.at[py], (gx, py))
        copy.wait_recv()
        copy.wait_send()
    sums = jnp.sum(parts_y[...], axis=0) - mine
    own = jnp.sum(jnp.where(sub_row == gy, sums, 0.0), axis=0, keepdims=True)
    resid_ref[...] = jnp.concatenate([own[:, :slots], own[:, slots : 2 * slots]], axis=0)


def on_device(nx, ny, prior, opening, courant, pulse, coords, instants, captured):
    kz2, kc2, small, kz00 = constants()
    dma = pltpu.SemaphoreType.DMA
    smem = pl.BlockSpec(memory_space=pltpu.SMEM)
    vmem = pl.BlockSpec(memory_space=pltpu.VMEM)
    hbm = pl.BlockSpec(memory_space=pl.ANY)
    return pl.pallas_call(
        functools.partial(kernel, nx, ny, kz00),
        out_shape=(
            jax.ShapeDtypeStruct(prior.shape, F32),
            jax.ShapeDtypeStruct(captured.shape, F32),
        ),
        in_specs=[hbm] * 6 + [smem] * 4,
        out_specs=(vmem, vmem),
        scratch_shapes=[
            pltpu.VMEM(prior.shape, BF16),
            pltpu.VMEM(prior.shape, BF16),
            pltpu.VMEM(prior.shape, BF16),
            pltpu.VMEM(kz2.shape, BF16),
            pltpu.VMEM(kc2.shape, BF16),
            pltpu.VMEM(small.shape, F32),
            pltpu.VMEM((2, SPAN, CX, LANES), F32),
            pltpu.VMEM((2, CY, HALO, LANES), F32),
            pltpu.VMEM((2, CY, HALO, LANES), F32),
            pltpu.VMEM((2, CY * CX, LANES), F32),
            pltpu.VMEM((ny, ny, LANES), F32),
            pltpu.VMEM((nx, ny, LANES), F32),
            pltpu.VMEM((2, SPAN, LANES), F32),
            pltpu.VMEM((2, CY, LANES), F32),
            pltpu.VMEM((2, CY, LANES), F32),
            pltpu.VMEM((nx, ny, LANES), F32),
            pltpu.VMEM((ny, ny, LANES), F32),
            pltpu.VMEM((nx, ny, LANES), F32),
            dma((6,)),
            dma((3, 4)),
            dma((3, 4)),
            dma((ny,)), dma((ny,)), dma((nx,)), dma((nx,)),
            dma((nx,)), dma((nx,)), dma((ny,)), dma((ny,)),
        ],
        compiler_params=pltpu.CompilerParams(
            collective_id=0, has_side_effects=True, vmem_limit_bytes=40 * 1024 * 1024
        ),
    )(
        prior, opening, courant, jnp.asarray(kz2), jnp.asarray(kc2), jnp.asarray(small),
        pulse, coords, instants, captured,
    )


def solution(mesh):
    placed = (
        P("gx", "gy"),
        P("gx", "gy"),
        P("gx", "gy"),
        P(),
        P(("gx", "gy"), None),
        P(("gx", "gy")),
        P(None, ("gx", "gy")),
    )
    return jax.shard_map(
        functools.partial(on_device, mesh.shape["gx"], mesh.shape["gy"]),
        mesh=mesh,
        in_specs=placed,
        out_specs=(P("gx", "gy"), P(None, ("gx", "gy"))),
        check_vma=False,
    )
```

```python
import functools

import jax
import jax.numpy as jnp
import ml_dtypes
import numpy as np
from jax import lax
from jax.experimental import pallas as pl
from jax.experimental.pallas import tpu as pltpu
from jax.sharding import PartitionSpec as P

CX = 24
CY = 24
HALO = 8
SPAN = 40
DEPTH = 256
LANES = 128
MESH = pl.DeviceIdType.MESH
HIGH = lax.Precision.HIGHEST
F32 = jnp.float32
BF16 = jnp.bfloat16


def constants():
    k = np.arange(SPAN)
    w = np.where(k <= SPAN // 2, k, k - SPAN)
    diff = k[:, None] - k[None, :]
    kx = np.einsum(
        "k,abk->ab",
        -((2 * np.pi * w / SPAN) ** 2) / SPAN,
        np.cos(2 * np.pi * diff[:, :, None] * k / SPAN),
    )
    kc = kx[HALO : HALO + CX]
    n = np.arange(DEPTH) + 1
    s = np.sqrt(2 / (DEPTH + 1)) * np.sin(np.pi / (DEPTH + 1) * (n[:, None] * n[None, :]))
    kz = (s * -((np.pi * n / (DEPTH + 1)) ** 2)) @ s.T

    def halves(a):
        hi = a.astype(ml_dtypes.bfloat16)
        return hi, (a - hi.astype(np.float64)).astype(ml_dtypes.bfloat16)

    kz2 = np.concatenate(halves(kz), axis=0)
    kc2 = np.concatenate(halves(kc), axis=0)
    small = np.zeros((24 + 3 * LANES + 8, DEPTH), np.float32)
    small[:CX, :SPAN] = kc
    taps = small[24 : 24 + 3 * LANES]
    taps[0:CX, :CX] = kc[:, HALO : HALO + CX].T
    taps[LANES + CX - HALO : LANES + CX, :CX] = kc[:, :HALO].T
    taps[2 * LANES : 2 * LANES + HALO, :CX] = kc[:, HALO + CX :].T
    small[24 + 3 * LANES :] = kz[0]
    return kz2, kc2, small, float(kz[0, 0])


def kernel(
    nx, ny, kz00,
    prior_hbm, opening_hbm, courant_hbm, kz_hbm, kc_hbm, small_hbm,
    pulse_hbm, coords_hbm, instants_hbm, captured_hbm,
    grad_ref, resid_ref,
    pulse, coords, instants, captured,
    prior, opening, courant, kz2, kc2, small,
    field, low_x, high_x, image,
    tiles, table, plane_ext, plane_low, plane_high, parts_x, parts_y, rec_out,
    load_sem, halo_send, halo_recv, ty_send, ty_recv, tx_send, tx_recv,
    rx_send, rx_recv, ry_send, ry_recv,
):
    gx, gy = lax.axis_index("gx"), lax.axis_index("gy")
    slots = instants.shape[0]
    rows = tiles.shape[1]

    loads = [
        pltpu.make_async_copy(src, dst, load_sem.at[i])
        for i, (src, dst) in enumerate(
            [
                (opening_hbm, opening), (kz_hbm, kz2), (kc_hbm, kc2),
                (prior_hbm, prior), (courant_hbm, courant), (small_hbm, small),
                (pulse_hbm, pulse), (coords_hbm, coords), (instants_hbm, instants),
                (captured_hbm, captured),
            ]
        )
    ]
    for load in loads:
        load.start()

    peers_y = [(gx, lax.rem(gy + k, ny)) for k in range(1, ny)]
    peers_x = [(lax.rem(gx + k, nx), gy) for k in range(1, nx)]
    barrier = pltpu.get_barrier_semaphore()
    for peer in peers_y + peers_x:
        pl.semaphore_signal(barrier, inc=1, device_id=peer, device_id_type=MESH)

    for load in loads[6:]:
        load.wait()

    lane_row = lax.broadcasted_iota(jnp.int32, (rows, LANES), 1)
    sub_row = lax.broadcasted_iota(jnp.int32, (rows, LANES), 0)
    mine = jnp.zeros((rows, LANES), F32)
    for j in range(slots):
        values = [
            captured[0, j], captured[1, j], (coords[0, j] + 1).astype(F32),
            coords[1, j].astype(F32), instants[j].astype(F32),
        ]
        for f, value in enumerate(values):
            mine = jnp.where(lane_row == f * slots + j, value, mine)
    tiles[gx] = jnp.where(sub_row == gx, mine, 0.0)

    loads[0].wait()
    for y in range(CY):
        for h in range(2):
            c0 = y * DEPTH + h * LANES
            field[h, HALO + y] = opening[:, c0 : c0 + LANES].astype(F32)

    pl.semaphore_wait(barrier, nx + ny - 2)

    def remote(src, dst, send, recv, peer):
        return pltpu.make_async_remote_copy(
            src_ref=src, dst_ref=dst, send_sem=send, recv_sem=recv,
            device_id=peer, device_id_type=MESH,
        )

    for px, _ in peers_x:
        remote(tiles.at[gx], tiles.at[gx], tx_send.at[px], tx_recv.at[gx], (px, gy)).start()

    ends = [
        (gy > 0, (gx, lax.max(gy - 1, 0))),
        (gy < ny - 1, (gx, lax.min(gy + 1, ny - 1))),
        (gx > 0, (lax.max(gx - 1, 0), gy)),
        (gx < nx - 1, (lax.min(gx + 1, nx - 1), gy)),
    ]

    def swap(stage, sources, targets):
        for i in (2, 3, 0, 1):
            there, peer = ends[i]

            @pl.when(there)
            def _():
                remote(
                    sources[i], targets[i ^ 1], halo_send.at[stage, i],
                    halo_recv.at[stage, i ^ 1], peer,
                ).start()

            @pl.when(jnp.logical_not(there))
            def _():
                targets[i][...] = jnp.zeros(targets[i].shape, F32)

        def finish(which=(0, 1, 2, 3)):
            for i in which:
                there, peer = ends[i]

                @pl.when(there)
                def _():
                    copy = remote(
                        sources[i], targets[i], halo_send.at[stage, i],
                        halo_recv.at[stage, i], peer,
                    )
                    copy.wait_recv()
                    copy.wait_send()

        return finish

    diag = (
        lax.broadcasted_iota(jnp.int32, (8, CX, LANES), 1)
        == lax.broadcasted_iota(jnp.int32, (8, CX, LANES), 2)
    )

    def to_plane(columns):
        return jnp.sum(jnp.where(diag, columns, 0.0), axis=1)


    def block(ref, b, h):
        return jnp.stack(
            [
                ref[:, y * DEPTH + h * LANES : y * DEPTH + (h + 1) * LANES].astype(F32)
                for y in range(8 * b, 8 * b + 8)
            ]
        )

    def top_plane(columns_of):
        return jnp.concatenate([to_plane(columns_of(b)[:, :, 0:1]) for b in range(3)], axis=0)

    def lateral_plane(stage, plane):
        ext, low, high = plane_ext.at[stage], plane_low.at[stage], plane_high.at[stage]
        ext[HALO : HALO + CY] = plane
        finish = swap(
            stage + 1,
            [
                ext.at[HALO : 2 * HALO], ext.at[CY : CY + HALO],
                ext.at[HALO : HALO + CY], ext.at[HALO : HALO + CY],
            ],
            [ext.at[0:HALO], ext.at[HALO + CY :], low, high],
        )

        def rest():
            finish()
            out = jnp.dot(small[:CX, :SPAN], ext[...], precision=HIGH, preferred_element_type=F32)
            wide = jnp.concatenate([plane, low[...], high[...]], axis=1)
            taps = small[24 : 24 + 3 * LANES, :LANES]
            return out + jnp.dot(wide, taps, precision=HIGH, preferred_element_type=F32)

        return rest

    loads[5].wait()
    kz_row = [small[24 + 3 * LANES : 25 + 3 * LANES, h * LANES : (h + 1) * LANES] for h in range(2)]
    p0 = top_plane(lambda b: field[0, HALO + 8 * b : 16 + 8 * b])
    finish_p0 = lateral_plane(0, p0)

    finish_halo = swap(
        0,
        [
            field.at[:, HALO : 2 * HALO], field.at[:, CY : CY + HALO],
            field.at[:, HALO : HALO + CY, 0:HALO], field.at[:, HALO : HALO + CY, CX - HALO : CX],
        ],
        [field.at[:, 0:HALO], field.at[:, HALO + CY :], low_x, high_x],
    )

    for px, _ in peers_x:
        copy = remote(tiles.at[gx], tiles.at[px], tx_send.at[px], tx_recv.at[px], (px, gy))
        copy.wait_recv()
        copy.wait_send()
    table[gy] = jnp.sum(tiles[...], axis=0)
    for _, py in peers_y:
        remote(table.at[gy], table.at[gy], ty_send.at[py], ty_recv.at[gy], (gx, py)).start()

    loads[1].wait()
    for b in range(3):
        pair = [field[h, HALO + 8 * b : 16 + 8 * b].reshape(8 * CX, LANES) for h in range(2)]
        lhs = jnp.concatenate(pair, axis=1).astype(BF16)
        out = jnp.dot(lhs, kz2[:DEPTH], preferred_element_type=F32)
        out = out + jnp.dot(lhs, kz2[DEPTH:], preferred_element_type=F32)
        for h in range(2):
            image[h, 8 * b * CX : 8 * (b + 1) * CX] = out[:, h * LANES : (h + 1) * LANES]

    for _, py in peers_y:
        copy = remote(table.at[gy], table.at[py], ty_send.at[py], ty_recv.at[py], (gx, py))
        copy.wait_recv()
        copy.wait_send()

    devices = rows * ny
    elements = table[...].reshape(devices, LANES)
    lane = lax.broadcasted_iota(jnp.int32, (devices, LANES), 1)
    first_hits, second_hits, spread = [], [], []
    group = lane // CY
    for j in range(slots):
        def column(f):
            return elements[:, f * slots + j : f * slots + j + 1]

        x = column(2).astype(jnp.int32) - 1 - gx * CX
        y = column(3).astype(jnp.int32) - gy * CY
        fires = column(4)
        first_hits.append(jnp.where((lane == x) & (lane < CX) & (column(2) > 0.0), 1.0, 0.0))
        second_hits.append(jnp.where((lane == y) & (lane < CY), 1.0, 0.0))
        weight = jnp.where(group == 0, jnp.where(fires == 0.0, pulse[0], 0.0), 0.0)
        weight = jnp.where(group == 1, jnp.where(fires == 1.0, pulse[1], 0.0), weight)
        weight = jnp.where(group == 2, 1.0, weight)
        weight = jnp.where(group == 3, column(0), weight)
        weight = jnp.where(group == 4, column(1), weight)
        inside = (lane - group * CY == y)
        spread.append(jnp.where(inside, weight, 0.0))
    first_hits = jnp.concatenate(first_hits, axis=0)
    second_hits = jnp.concatenate(second_hits, axis=0)
    planes = lax.dot_general(
        jnp.concatenate(spread, axis=0), first_hits, (((0,), (0,)), ((), ())),
        precision=HIGH, preferred_element_type=F32,
    )
    source_0, source_1, hits, seen_0, seen_1 = [planes[CY * i : CY * (i + 1)] for i in range(5)]


    loads[3].wait()
    loads[4].wait()
    c0 = top_plane(lambda b: block(courant, b, 0))
    before = top_plane(lambda b: block(prior, b, 0))
    im0 = top_plane(
        lambda b: image[0, 8 * b * CX : 8 * (b + 1) * CX].reshape(8, CX, LANES)
    ) + finish_p0()
    p1 = 2.0 * p0 - before + c0 * im0 + source_0
    lateral_1 = lateral_plane(1, p1)()
    loads[2].wait()

    flat = field.reshape(2, SPAN * CX, LANES)
    kc = kc2[...]

    def lateral(window):
        out = jnp.dot(kc, window.astype(BF16), preferred_element_type=F32)
        return out[:CX] + out[CX:]

    def both(x):
        window = jnp.concatenate(
            [flat[h, pl.ds(x, SPAN, stride=CX), :] for h in range(2)], axis=1
        )
        out = lateral(window)
        for h in range(2):
            at = (h, pl.ds(x, CY, stride=CX), slice(None))
            image[at] = image[at] + out[:, h * LANES : (h + 1) * LANES]

    def first(y):
        window = jnp.concatenate(
            [
                jnp.concatenate([low_x[h, y], field[h, HALO + y], high_x[h, y]], axis=0)
                for h in range(2)
            ],
            axis=1,
        )
        out = lateral(window)
        for h in range(2):
            image[h, CX * y : CX * (y + 1)] += out[:, h * LANES : (h + 1) * LANES]

    finish_halo((0, 1))
    for i in range(CX):
        both(i)
    finish_halo((2, 3))
    for i in range(CY):
        first(i)

    depth1 = []
    for b in range(3):
        total = jnp.zeros((8, CX, LANES), F32)
        for h in range(2):
            now = field[h, HALO + 8 * b : 16 + 8 * b]
            im = image[h, 8 * b * CX : 8 * (b + 1) * CX].reshape(8, CX, LANES)
            newest = 2.0 * now - block(prior, b, h) + block(courant, b, h) * im
            total = total + newest * kz_row[h]
        depth1.append(to_plane(jnp.sum(total, axis=2, keepdims=True)))
    depth1 = jnp.concatenate(depth1, axis=0)
    depth1 = depth1 + kz00 * source_0

    im1 = lateral_1 + depth1
    p2 = 2.0 * p1 - p0 + c0 * im1 + source_1
    a1 = hits * p2 - seen_1
    inject_0 = hits * p1 - seen_0
    finish_a1 = lateral_plane(2, a1)

    records = jnp.zeros((devices, LANES), F32)
    for t, plane in enumerate((p1, p2)):
        picked = jnp.dot(second_hits[:, :CY], plane, precision=HIGH, preferred_element_type=F32)
        picked = jnp.sum(picked * first_hits, axis=1, keepdims=True)
        for j in range(slots):
            records = jnp.where(
                lane == t * slots + j, picked[j * devices : (j + 1) * devices], records
            )
    rec_out[...] = records.reshape(ny, rows, LANES)
    parts_y[gy] = rec_out[gy]
    for _, py in peers_y:
        remote(rec_out.at[py], parts_y.at[gy], ry_send.at[py], ry_recv.at[gy], (gx, py)).start()

    for b in range(3):
        columns = jnp.sum(
            jnp.where(diag, a1[8 * b : 8 * b + 8].reshape(8, 1, LANES), 0.0), axis=2, keepdims=True
        )
        for i in range(8):
            y = 8 * b + i
            for h in range(2):
                at = (slice(None), slice(y * DEPTH + h * LANES, y * DEPTH + (h + 1) * LANES))
                grad_ref[at] = (
                    courant[at].astype(F32) * (columns[i] * kz_row[h])
                    * image[h, y * CX : (y + 1) * CX]
                )

    for _, py in peers_y:
        copy = remote(rec_out.at[py], parts_y.at[py], ry_send.at[py], ry_recv.at[py], (gx, py))
        copy.wait_recv()
        copy.wait_send()
    parts_x[gx] = jnp.sum(parts_y[...], axis=0)
    for px, _ in peers_x:
        remote(parts_x.at[gx], parts_x.at[gx], rx_send.at[px], rx_recv.at[gx], (px, gy)).start()

    more = (2.0 * a1 + c0 * finish_a1() + inject_0) * im0 + a1 * im1
    top = lax.broadcasted_iota(jnp.int32, (CX, LANES), 1) == 0
    for b in range(3):
        columns = jnp.sum(
            jnp.where(diag, more[8 * b : 8 * b + 8].reshape(8, 1, LANES), 0.0),
            axis=2, keepdims=True,
        )
        for i in range(8):
            at = (slice(None), slice((8 * b + i) * DEPTH, (8 * b + i) * DEPTH + LANES))
            grad_ref[at] = grad_ref[at] + jnp.where(top, columns[i], 0.0)

    for px, _ in peers_x:
        copy = remote(parts_x.at[gx], parts_x.at[px], rx_send.at[px], rx_recv.at[px], (px, gy))
        copy.wait_recv()
        copy.wait_send()
    sums = jnp.sum(parts_x[...], axis=0) - mine
    own = jnp.sum(jnp.where(sub_row == gx, sums, 0.0), axis=0, keepdims=True)
    resid_ref[...] = jnp.concatenate([own[:, :slots], own[:, slots : 2 * slots]], axis=0)


def on_device(nx, ny, prior, opening, courant, pulse, coords, instants, captured):
    kz2, kc2, small, kz00 = constants()
    coords = coords.T
    rows = -(-nx // 8) * 8
    dma = pltpu.SemaphoreType.DMA
    vmem = pl.BlockSpec(memory_space=pltpu.VMEM)
    hbm = pl.BlockSpec(memory_space=pltpu.HBM)
    return pl.pallas_call(
        functools.partial(kernel, nx, ny, kz00),
        out_shape=(
            pltpu.VMEM(prior.shape, F32),
            pltpu.VMEM(captured.shape, F32),
        ),
        in_specs=[hbm] * 10,
        out_specs=(vmem, vmem),
        scratch_shapes=[
            pltpu.SMEM(pulse.shape, F32),
            pltpu.SMEM(coords.shape, jnp.int32),
            pltpu.SMEM(instants.shape, jnp.int32),
            pltpu.SMEM(captured.shape, F32),
            pltpu.VMEM(prior.shape, BF16),
            pltpu.VMEM(prior.shape, BF16),
            pltpu.VMEM(prior.shape, BF16),
            pltpu.VMEM(kz2.shape, BF16),
            pltpu.VMEM(kc2.shape, BF16),
            pltpu.VMEM(small.shape, F32),
            pltpu.VMEM((2, SPAN, CX, LANES), F32),
            pltpu.VMEM((2, CY, HALO, LANES), F32),
            pltpu.VMEM((2, CY, HALO, LANES), F32),
            pltpu.VMEM((2, CY * CX, LANES), F32),
            pltpu.VMEM((nx, rows, LANES), F32),
            pltpu.VMEM((ny, rows, LANES), F32),
            pltpu.VMEM((3, SPAN, LANES), F32),
            pltpu.VMEM((3, CY, LANES), F32),
            pltpu.VMEM((3, CY, LANES), F32),
            pltpu.VMEM((nx, rows, LANES), F32),
            pltpu.VMEM((ny, rows, LANES), F32),
            pltpu.VMEM((ny, rows, LANES), F32),
            dma((10,)),
            dma((4, 4)),
            dma((4, 4)),
            dma((ny,)), dma((ny,)), dma((nx,)), dma((nx,)),
            dma((nx,)), dma((nx,)), dma((ny,)), dma((ny,)),
        ],
        compiler_params=pltpu.CompilerParams(
            collective_id=0, has_side_effects=True, vmem_limit_bytes=62 * 1024 * 1024
        ),
    )(
        prior, opening, courant, jnp.asarray(kz2), jnp.asarray(kc2), jnp.asarray(small),
        pulse, coords, instants, captured,
    )


def solution(mesh):
    placed = (
        P("gx", "gy"),
        P("gx", "gy"),
        P("gx", "gy"),
        P(),
        P(("gx", "gy"), None),
        P(("gx", "gy")),
        P(None, ("gx", "gy")),
    )
    return jax.shard_map(
        functools.partial(on_device, mesh.shape["gx"], mesh.shape["gy"]),
        mesh=mesh,
        in_specs=placed,
        out_specs=(P("gx", "gy"), P(None, ("gx", "gy"))),
        check_vma=False,
    )
```
